32 devices in a mesh: dp: 4 (over z), expert: 4 (over y, core), etensor: 2 (over x).
Axes of the slice: x: 2, y: 2, z: 4, core: 2. Of those that a mesh axis runs over, the one named last changes fastest.
Arguments:
- token_rows: bfloat16 [2048, 4096], P(('dp', 'expert')), may hold values from -6 to 6
- row_grads: bfloat16 [2048, 4096], P(('dp', 'expert')), may hold values from -6 to 6
- gate_scale: bfloat16 [2048], P(('dp', 'expert')), may hold values from 0.099609375 to 1
- routing: int32 [2048, 1], P(('dp', 'expert')), may hold values from 0 to 3; in each aligned block of 128 rows (0 to 127, 128 to 255, ...) at most 48 rows name the same one
- gate_weight: bfloat16 [4, 14336, 4096], P('expert', ('dp', 'etensor')), may hold values from -0.09375 to 0.09375
- up_weight: bfloat16 [4, 14336, 4096], P('expert', ('dp', 'etensor')), may hold values from -0.09375 to 0.09375
- down_weight: bfloat16 [4, 14336, 4096], P('expert', ('dp', 'etensor')), may hold values from -0.046875 to 0.046875
Outputs:
- input_grads: bfloat16 [2048, 4096], P(('dp', 'expert'))
- scale_grads: float32 [2048], P(('dp', 'expert'))
- grad_gate_weight: bfloat16 [4, 14336, 4096], P('expert', ('dp', 'etensor'))
- grad_up_weight: bfloat16 [4, 14336, 4096], P('expert', ('dp', 'etensor'))
- grad_down_weight: bfloat16 [4, 14336, 4096], P('expert', ('dp', 'etensor'))
The draws below stay inside these ranges and needn't reach their ends.
Inputs may be any that keep to these rules, and one draw needn't show every extreme that they name: `routing`: among the 128 rows of one aligned block (the rows of one index of dp and expert) no expert is named more than 48 times.
All inputs are finite; a program needn't handle non-finite values.
Results may differ from the reference program's by a relative error of at most 0.0057.
Values may be sent and summed in bfloat16 or wider, within the bound.
No kernel may reach another device: no remote copies, remote signals or barrier semaphores. Data moves between devices by JAX's collectives and lax.ppermute only.
A program may use at most 256 MiB of HBM per device.

```python
import math
import jax
import jax.numpy as jnp
import numpy as np

D = 4096
FF = 14336
ROWS_DEV = 128
CAP = 48
EXPERTS = 4
ROWS = 2048
N_DP = 4
N_EXPERT = 4


def level_of(own_key, dims, pieces, least, high):
    level, own = 1.0, jax.random.fold_in(own_key, 6)
    for dim, shards_of in pieces:
        heights = jnp.exp(jax.random.uniform(jax.random.fold_in(own, dim), (shards_of,), jnp.float32, least / len(pieces), high / len(pieces)))
        level = level * jnp.repeat(heights, dims[dim] // shards_of).reshape([-1 if axis == dim else 1 for axis in range(len(dims))])
    return level


def deal_out(own_key, own, number, rows, number_of, top, most, skew):
    ranking = jax.random.permutation(own_key, number_of)
    crowded, usual = shares(number_of, rows * top, most, skew, True), shares(number_of, rows * top, most, skew, False)
    places = jnp.arange(number_of)

    def named(sizes, rotation):
        used = int((sizes > 0).sum())
        fixed = max(1, used // 4)
        passed = fixed + (places - fixed + rotation * (used - fixed)) % max(1, number_of - fixed)
        return jnp.zeros((number_of,), jnp.int32).at[ranking[jnp.where(places < fixed, places, passed)]].set(jnp.asarray(sizes, jnp.int32))

    sizes = jnp.where(number % 4 == 0, named(crowded, number // 4), named(usual, number - number // 4 - 1))
    mixed = jax.random.permutation(jax.random.fold_in(own, 3), number_of)
    source_of, receiver = mixed[0:number_of // 2 * 2:2], mixed[1:number_of // 2 * 2:2]
    slack = jnp.minimum(sizes[source_of] - 1, most - sizes[receiver]) // 2
    slack = jnp.where((source_of == ranking[0]) | (receiver == ranking[0]) | (sizes[receiver] == 0), 0, jnp.maximum(slack, 0))
    passed = jax.random.randint(jax.random.fold_in(own, 4), (number_of // 2,), 0, 1 << 20) % (slack + 1)
    sizes = sizes.at[source_of].add(-passed).at[receiver].add(passed)
    members = jnp.searchsorted(jnp.cumsum(sizes), jnp.arange(rows * top), side="right").astype(jnp.int32)
    table = members.reshape(top, rows).T
    table = table[jax.random.permutation(jax.random.fold_in(own, 1), rows)]
    rotation = jax.random.randint(jax.random.fold_in(own, 2), (rows, 1), 0, top)
    return jnp.take_along_axis(table, (jnp.arange(top)[None, :] + rotation) % top, axis=1)


def shares(count, total, most, skew, full):
    portions = [(1 << 20) // math.isqrt(grade ** skew) + 1 for grade in range(1, count + 1)]
    largest = most if full else min(most, max(-(-total // count), total * portions[0] // sum(portions)))
    least = 1 if total - largest >= count - 1 else 0
    given, rest = [largest] + [least] * (count - 1), total - largest - least * (count - 1)
    while rest > 0:
        candidates = [i for i in range(1, count) if given[i] < largest] or [i for i in range(1, count) if given[i] < most]
        mass, left = sum([portions[i] for i in candidates]), rest
        for i in candidates:
            more = min(most - given[i], max(1, left * portions[i] // mass), rest)
            given[i] = given[i] + more
            rest = rest - more
    return np.array(given)


def gaussian(rng, dims, spread, bound, cuts=(), dtype=jnp.bfloat16):
    drawn = spread * jax.random.normal(rng, dims, jnp.float32)
    if cuts:
        drawn = drawn * level_of(rng, dims, cuts, -0.22, 0.18)
    return jnp.clip(drawn, -bound, bound).astype(dtype)


def setup_inputs(seed: int = 0) -> dict:
    splits = jax.random.split(jax.random.key(seed), 8)
    token_rows = gaussian(splits[0], (ROWS, D), 1.0, 6.0, ((0, 16),))
    row_grads = gaussian(splits[1], (ROWS, D), 1.0, 6.0, ((0, 16),))
    gate_scale = jnp.clip(0.099609375 + 0.9003906 * jax.random.uniform(splits[2], (ROWS,), jnp.float32) ** level_of(splits[2], (ROWS,), ((0, 16),), -0.2, 0.2), 0.099609375, 1.0).astype(jnp.bfloat16)
    routing_keys = jax.random.split(jax.random.fold_in(splits[3], 1), ROWS // ROWS_DEV)
    routing_turns = jax.random.permutation(jax.random.fold_in(splits[3], 3), ROWS // ROWS_DEV)
    routing = jax.vmap(lambda own, number: deal_out(jax.random.fold_in(splits[3], 2), own, number, ROWS_DEV, EXPERTS, 1, CAP, 2))(routing_keys, routing_turns).reshape((ROWS, 1))
    gate_weight = gaussian(splits[4], (EXPERTS, FF, D), D ** -0.5, 0.09375, ((0, 4), (1, 8)))
    up_weight = gaussian(splits[5], (EXPERTS, FF, D), D ** -0.5, 0.09375, ((0, 4), (1, 8)))
    down_weight = gaussian(splits[6], (EXPERTS, FF, D), FF ** -0.5, 0.046875, ((0, 4), (1, 8)))
    return dict(token_rows=token_rows, row_grads=row_grads, gate_scale=gate_scale, routing=routing, gate_weight=gate_weight, up_weight=up_weight, down_weight=down_weight)


def reference(token_rows, row_grads, gate_scale, routing, gate_weight, up_weight, down_weight):
    route = routing[:, 0]
    limit = CAP * N_DP * N_EXPERT
    input_grads = jnp.zeros((ROWS, D), jnp.bfloat16)
    scale_grads = jnp.zeros((ROWS,), jnp.float32)
    grads_gate = []
    grads_up = []
    grads_down = []
    for expert_id in range(EXPERTS):
        picked = jnp.nonzero(route == expert_id, size=limit, fill_value=ROWS)[0].astype(jnp.int32)
        picked_rows = jnp.take(token_rows, picked, axis=0, mode="fill", fill_value=0)
        picked_grads = jnp.take(row_grads, picked, axis=0, mode="fill", fill_value=0)
        picked_scale = jnp.take(gate_scale, picked, axis=0, mode="fill", fill_value=0).astype(jnp.float32)
        w_gate = gate_weight[expert_id]
        w_up = up_weight[expert_id]
        w_down = down_weight[expert_id]
        gate_pre = jnp.dot(picked_rows, w_gate.T, preferred_element_type=jnp.float32)
        up_pre = jnp.dot(picked_rows, w_up.T, preferred_element_type=jnp.float32)
        sigmoid_gate = jax.nn.sigmoid(gate_pre)
        activated = gate_pre * sigmoid_gate
        hidden = (activated * up_pre).astype(jnp.bfloat16)
        hidden_raw = jnp.dot(picked_grads, w_down.T, preferred_element_type=jnp.float32)
        scale_part = jnp.sum(hidden.astype(jnp.float32) * hidden_raw, axis=1)
        hidden_grad = picked_scale[:, None] * hidden_raw
        gate_pre_grad = (hidden_grad * up_pre * sigmoid_gate * (1.0 + gate_pre * (1.0 - sigmoid_gate))).astype(jnp.bfloat16)
        up_pre_grad = (hidden_grad * activated).astype(jnp.bfloat16)
        scaled_grads = (picked_scale[:, None] * picked_grads.astype(jnp.float32)).astype(jnp.bfloat16)
        grads_gate.append(jnp.dot(gate_pre_grad.T, picked_rows, preferred_element_type=jnp.float32).astype(jnp.bfloat16))
        grads_up.append(jnp.dot(up_pre_grad.T, picked_rows, preferred_element_type=jnp.float32).astype(jnp.bfloat16))
        grads_down.append(jnp.dot(hidden.T, scaled_grads, preferred_element_type=jnp.float32).astype(jnp.bfloat16))
        row_part = jnp.dot(gate_pre_grad, w_gate, preferred_element_type=jnp.float32) + jnp.dot(up_pre_grad, w_up, preferred_element_type=jnp.float32)
        input_grads = input_grads.at[picked].set(row_part.astype(jnp.bfloat16), mode="drop")
        scale_grads = scale_grads.at[picked].set(scale_part, mode="drop")
    return input_grads, scale_grads, jnp.stack(grads_gate), jnp.stack(grads_up), jnp.stack(grads_down)
```

```python
import functools

import jax
import jax.numpy as jnp
from jax import lax
from jax.experimental import pallas as pl
from jax.experimental.pallas import tpu as pltpu
from jax.sharding import PartitionSpec as P

LANES = 128
F_BLOCK = 256
MIB = 1 << 20
VMEM = 56 * MIB
SMALL = pl.CostEstimate(flops=0, bytes_accessed=0, transcendentals=0)

OUTER = ((0, 1), (1, 0), (2, 3), (3, 2))
MIDDLE = ((1, 2), (2, 1))
OUT = ((1, 0), (2, 3))
IN = ((0, 1), (3, 2))
SKIP = ((0, 2), (2, 0), (1, 3), (3, 1))
ENDS = ((0, 3), (3, 0))
IN_TWO = ((0, 2), (3, 1))
OUT_TWO = ((2, 0), (1, 3))


def nt_dot(a, b):
    return lax.dot_general(a, b, (((1,), (1,)), ((), ())), preferred_element_type=jnp.float32)


def tn_dot(a, b):
    return lax.dot_general(a, b, (((0,), (0,)), ((), ())), preferred_element_type=jnp.float32)


def pack_kernel(slot_ref, rows_ref, grads_ref, scale_ref, *out_refs):
    width = rows_ref.shape[1]
    slot = slot_ref[...]
    for group, out_ref in enumerate(out_refs):
        size = out_ref.shape[0]
        at = lax.broadcasted_iota(jnp.int32, (size, slot.shape[1]), 0) + group * size
        placing = (at == slot).astype(jnp.float32).astype(jnp.bfloat16)
        for start, ref in ((0, rows_ref), (width, grads_ref), (2 * width, scale_ref)):
            out_ref[:, start : start + ref.shape[1]] = jnp.dot(
                placing, ref[...], preferred_element_type=jnp.float32
            ).astype(jnp.bfloat16)


def pack(slot, rows, grads, scale, groups, size):
    width = rows.shape[1]
    shape = jax.ShapeDtypeStruct((size, 2 * width + LANES), jnp.bfloat16)
    return pl.pallas_call(
        pack_kernel,
        out_shape=[shape] * groups,
        compiler_params=pltpu.CompilerParams(vmem_limit_bytes=32 * MIB),
        cost_estimate=pl.CostEstimate(
            flops=2 * groups * size * rows.shape[0] * 2 * width,
            bytes_accessed=4 * (rows.shape[0] + groups * size) * width,
            transcendentals=0,
        ),
    )(slot, rows, grads, scale)


class Order:
    def __init__(self):
        self.token = jnp.zeros((8, LANES), jnp.float32)

    def call(self, kernel, operands, in_specs, out_shape, out_specs, **options):
        n_in, n_out = len(operands), len(out_shape)

        def body(*refs):
            ins, refs = refs[:n_in], refs[n_in + 1 :]
            outs, scratch = refs[:n_out], refs[n_out + 1 :]
            kernel(*ins, *outs, *scratch)

        anywhere = pl.BlockSpec(memory_space=pl.ANY)
        *out, self.token = pl.pallas_call(
            body,
            in_specs=[*in_specs, anywhere],
            out_specs=[*out_specs, anywhere],
            out_shape=[*out_shape, jax.ShapeDtypeStruct(self.token.shape, self.token.dtype)],
            input_output_aliases={n_in: n_out},
            compiler_params=pltpu.CompilerParams(vmem_limit_bytes=VMEM),
            cost_estimate=SMALL,
            **options,
        )(*operands, self.token)
        return out


def choose_kernel(picks, copies, needs, flag_ref, *refs):
    n_in = 2 * picks + copies
    ins, outs = refs[:n_in], refs[n_in + needs : -1]
    sems = refs[-1]

    def move(first):
        pairs = [(ins[2 * i + 1 - first], outs[i]) for i in range(picks)]
        pairs += [(ins[2 * picks + i], outs[picks + i]) for i in range(copies)]
        moves = [pltpu.make_async_copy(a, b, sems.at[i]) for i, (a, b) in enumerate(pairs)]
        for one in moves:
            one.start()
        for one in moves:
            one.wait()

    @pl.when(flag_ref[0] == 1)
    def _():
        move(1)

    @pl.when(flag_ref[0] != 1)
    def _():
        move(0)


def choose(order, flag, pairs, singles=(), needs=()):
    operands = [flag, *[a for pair in pairs for a in pair], *singles, *needs]
    anywhere = pl.BlockSpec(memory_space=pl.ANY)
    out_shape = [jax.ShapeDtypeStruct(a.shape, a.dtype) for a in [p[0] for p in pairs] + list(singles)]
    return order.call(
        functools.partial(choose_kernel, len(pairs), len(singles), len(needs)),
        operands,
        [pl.BlockSpec(memory_space=pltpu.SMEM)] + [anywhere] * (len(operands) - 1),
        out_shape,
        [anywhere] * len(out_shape),
        scratch_shapes=[pltpu.SemaphoreType.DMA((len(out_shape),))],
    )


def sum_kernel(plan, flag_ref, *refs):
    n_in = len(refs) - len(plan)
    for (rows, terms, others), out_ref in zip(plan, refs[n_in:], strict=True):

        def add(terms, out_ref=out_ref, rows=rows):
            total = None
            for k, start in terms:
                term = refs[k][start : start + rows, :].astype(jnp.float32)
                total = term if total is None else total + term
            out_ref[...] = total.astype(out_ref.dtype)

        if others is None:
            add(terms)
        else:
            pl.when(flag_ref[0] == 1)(functools.partial(add, terms))
            pl.when(flag_ref[0] != 1)(functools.partial(add, others))


def sums(order, flag, operands, plan):
    width = operands[0].shape[1]
    inside = pl.BlockSpec(memory_space=pltpu.VMEM)
    return order.call(
        functools.partial(sum_kernel, plan),
        [flag, *operands],
        [pl.BlockSpec(memory_space=pltpu.SMEM)] + [inside] * len(operands),
        [jax.ShapeDtypeStruct((rows, width), jnp.bfloat16) for rows, _, _ in plan],
        [inside] * len(plan),
    )


def unit_kernel(n_pieces, parts, count, lane_ref, flag_ref, *refs):
    pieces = refs[:n_pieces]
    weights = refs[n_pieces : n_pieces + 3]
    refs = refs[n_pieces + 3 :]
    outs, scaled_out = refs[:3], refs[3]
    partial_refs = refs[4 : 4 + len(parts)]
    (
        rows_ref,
        grads_ref,
        scale_ref,
        scaled_ref,
        total_ref,
        scale_sum_ref,
        held_ref,
        act_ref,
        piece_sems,
        weight_sems,
        act_sems,
        scaled_sem,
    ) = refs[4 + len(parts) :]
    size = pieces[0].shape[0]
    width = rows_ref.shape[1]
    slots = held_ref.shape[0]

    def weight_copy(i, k):
        return pltpu.make_async_copy(
            weights[k].at[pl.ds(i * F_BLOCK, F_BLOCK), :],
            held_ref.at[lax.rem(i, slots), k],
            weight_sems.at[lax.rem(i, slots), k],
        )

    def act_copy(i, k):
        return pltpu.make_async_copy(
            act_ref.at[lax.rem(i, 2), k],
            outs[k].at[:, pl.ds(pl.multiple_of(i * F_BLOCK, F_BLOCK), F_BLOCK)],
            act_sems.at[lax.rem(i, 2), k],
        )

    def piece_copies(j, start, ref):
        return [
            pltpu.make_async_copy(
                piece.at[:, pl.ds(start, ref.shape[1])],
                ref.at[pl.ds(i * size, size), :],
                piece_sems.at[i, j],
            )
            for i, piece in enumerate(pieces)
        ]

    row_copies = piece_copies(0, 0, rows_ref)
    grad_copies = piece_copies(1, width, grads_ref) + piece_copies(2, 2 * width, scale_ref)
    for copy in row_copies:
        copy.start()
    weight_copy(0, 0).start()
    weight_copy(0, 1).start()
    for copy in grad_copies:
        copy.start()
    weight_copy(0, 2).start()
    for k in range(3):
        weight_copy(1, k).start()
    total_ref[...] = jnp.zeros_like(total_ref)
    scale_sum_ref[...] = jnp.zeros_like(scale_sum_ref)
    for copy in row_copies + grad_copies:
        copy.wait()
    scale = scale_ref[:, 0:1].astype(jnp.float32)
    scaled_ref[...] = (scale * grads_ref[...].astype(jnp.float32)).astype(jnp.bfloat16)
    scaled_copy = pltpu.make_async_copy(scaled_ref, scaled_out, scaled_sem)
    scaled_copy.start()

    def products(i):
        held = held_ref.at[lax.rem(i, slots)]
        gate_pre = nt_dot(rows_ref[...], held[0])
        up_pre = nt_dot(rows_ref[...], held[1])
        raw = nt_dot(grads_ref[...], held[2])
        return gate_pre, up_pre, raw

    def activate(i, gate_pre, up_pre, raw):
        sigmoid = jax.nn.sigmoid(gate_pre)
        activated = gate_pre * sigmoid
        hidden = (activated * up_pre).astype(jnp.bfloat16)
        scale_sum_ref[...] += jnp.sum(hidden.astype(jnp.float32) * raw, axis=1, keepdims=True)
        hidden_grad = scale_ref[:, 0:1].astype(jnp.float32) * raw
        act = act_ref.at[lax.rem(i, 2)]
        act[0] = hidden
        act[1] = (
            hidden_grad * up_pre * sigmoid * (1.0 + gate_pre * (1.0 - sigmoid))
        ).astype(jnp.bfloat16)
        act[2] = (hidden_grad * activated).astype(jnp.bfloat16)

    def add_inputs(i, finish=None):
        held = held_ref.at[lax.rem(i, slots)]
        act = act_ref.at[lax.rem(i, 2)]
        gate_grad, up_grad = act[1], act[2]
        tile = 1024
        for start in range(0, width, tile):
            at = slice(start, start + tile)
            total = (
                total_ref[:, at]
                + jnp.dot(gate_grad, held[0, :, at], preferred_element_type=jnp.float32)
                + jnp.dot(up_grad, held[1, :, at], preferred_element_type=jnp.float32)
            )
            if finish is None:
                total_ref[:, at] = total
            else:
                finish(at, total)

    def arrive(i):
        for k in range(3):
            weight_copy(i, k).wait()

        @pl.when(i + 2 < count)
        def _():
            for k in range(3):
                weight_copy(i + 2, k).start()

    arrive(0)
    activate(0, *products(0))
    for k in range(3):
        act_copy(0, k).start()

    def step(i, carry):
        arrive(i)

        @pl.when(i >= 2)
        def _():
            for k in range(3):
                act_copy(i - 2, k).wait()

        now = products(i)
        add_inputs(i - 1)
        activate(i, *now)
        for k in range(3):
            act_copy(i, k).start()
        return carry

    lax.fori_loop(1, count, step, 0)

    def write(at, value):
        for ref, (start, size, other) in zip(partial_refs, parts, strict=True):
            part = value[start : start + size].astype(jnp.bfloat16)
            if other is None:
                ref[:, at] = part
            else:
                second = value[other : other + size].astype(jnp.bfloat16)
                ref[:, at] = jnp.where(flag_ref[0] == 1, part, second)

    add_inputs(count - 1, write)
    value = scale_sum_ref[...]
    high = value.astype(jnp.bfloat16).astype(jnp.float32)
    lane = lax.broadcasted_iota(jnp.int32, (value.shape[0], LANES), 1)
    first = lane_ref[0]
    lanes = jnp.where(lane == first, high, jnp.where(lane == first + 1, value - high, 0.0))
    write(slice(width, width + LANES), lanes)
    for i in (count - 2, count - 1):
        for k in range(3):
            act_copy(i, k).wait()
    scaled_copy.wait()


class Unit:
    def __init__(self, order, lane, flag, pieces, parts, weights):
        size = pieces[0].shape[0]
        rows = size * len(pieces)
        units, width = weights[0].shape
        count = units // F_BLOCK
        anywhere = pl.BlockSpec(memory_space=pl.ANY)
        inside = pl.BlockSpec(memory_space=pltpu.VMEM)
        scalar = pl.BlockSpec(memory_space=pltpu.SMEM)
        bf16 = jnp.bfloat16
        out = order.call(
            functools.partial(unit_kernel, len(pieces), parts, count),
            [lane, flag, *pieces, *weights],
            [scalar, scalar] + [anywhere] * (len(pieces) + 3),
            [jax.ShapeDtypeStruct((rows, units), bf16)] * 3
            + [jax.ShapeDtypeStruct((rows, width), bf16)]
            + [jax.ShapeDtypeStruct((part[1], width + LANES), bf16) for part in parts],
            [anywhere] * 4 + [inside] * len(parts),
            scratch_shapes=[
                pltpu.VMEM((rows, width), bf16),
                pltpu.VMEM((rows, width), bf16),
                pltpu.VMEM((rows, LANES), bf16),
                pltpu.VMEM((rows, width), bf16),
                pltpu.VMEM((rows, width), jnp.float32),
                pltpu.VMEM((rows, 1), jnp.float32),
                pltpu.VMEM((4, 3, F_BLOCK, width), bf16),
                pltpu.VMEM((2, 3, rows, F_BLOCK), bf16),
                pltpu.SemaphoreType.DMA((len(pieces), 3)),
                pltpu.SemaphoreType.DMA((4, 3)),
                pltpu.SemaphoreType.DMA((2, 3)),
                pltpu.SemaphoreType.DMA(()),
            ],
        )
        self.hidden, self.gate_grad, self.up_grad, self.scaled = out[:4]
        self.partials = out[4:]
        self.pieces = pieces


def weight_kernel(n_right, n_left, *refs):
    right, refs = refs[:n_right], refs[n_right:]
    left, refs = refs[:n_left], refs[n_left:]
    out_ref, rows_ref, sems = refs
    width = rows_ref.shape[1]

    @pl.when(pl.program_id(0) == 0)
    def _():
        copies, start = [], 0
        for i, ref in enumerate(right):
            size = ref.shape[0]
            copies.append(
                pltpu.make_async_copy(
                    ref.at[:, pl.ds(0, width)], rows_ref.at[pl.ds(start, size), :], sems.at[i]
                )
            )
            start += size
        for copy in copies:
            copy.start()
        for copy in copies:
            copy.wait()

    both = jnp.concatenate([ref[...] for ref in left], axis=0)
    tile = 1024
    for start in range(0, width, tile):
        at = slice(start, start + tile)
        out_ref[:, at] = tn_dot(both, rows_ref[:, at]).astype(jnp.bfloat16)


def weight_grad(order, right, left, width):
    rows = sum(a.shape[0] for a in left)
    units = left[0].shape[1]
    anywhere = pl.BlockSpec(memory_space=pl.ANY)
    return order.call(
        functools.partial(weight_kernel, len(right), len(left)),
        [*right, *left],
        [anywhere] * len(right)
        + [pl.BlockSpec((a.shape[0], F_BLOCK), lambda i: (0, i)) for a in left],
        [jax.ShapeDtypeStruct((units, width), jnp.bfloat16)],
        [pl.BlockSpec((F_BLOCK, width), lambda i: (i, 0))],
        grid=(units // F_BLOCK,),
        scratch_shapes=[
            pltpu.VMEM((rows, width), jnp.bfloat16),
            pltpu.SemaphoreType.DMA((len(right),)),
        ],
    )[0]


def unpack_kernel(slot_ref, *refs):
    grads_ref, scale_ref = refs[-2:]
    width = grads_ref.shape[1]
    slot = slot_ref[...]
    total = jnp.zeros((slot.shape[0], width + LANES), jnp.float32)
    for group, ref in enumerate(refs[:-2]):
        size = ref.shape[0]
        at = lax.broadcasted_iota(jnp.int32, (slot.shape[0], size), 1) + group * size
        placing = (at == slot).astype(jnp.float32).astype(jnp.bfloat16)
        total += jnp.dot(placing, ref[...], preferred_element_type=jnp.float32)
    grads_ref[...] = total[:, :width].astype(jnp.bfloat16)
    scale_ref[...] = jnp.sum(total[:, width:], axis=1, keepdims=True)


def unpack(order, slot, groups, width):
    rows = slot.shape[0]
    inside = pl.BlockSpec(memory_space=pltpu.VMEM)
    return order.call(
        unpack_kernel,
        [slot, *groups],
        [inside] * (1 + len(groups)),
        [
            jax.ShapeDtypeStruct((rows, width), jnp.bfloat16),
            jax.ShapeDtypeStruct((rows, 1), jnp.float32),
        ],
        [inside] * 2,
    )


def line_device(token_rows, row_grads, gate_scale, routing, gate_weight, up_weight, down_weight):
    width = token_rows.shape[1]
    local_rows = token_rows.shape[0]
    size = 3 * local_rows // 8
    z, e, x = (lax.axis_index(name) for name in ("dp", "expert", "etensor"))
    middle = (z == 1) | (z == 2)
    w_gate, w_up, w_down = gate_weight[0], up_weight[0], down_weight[0]
    lane = ((z * 2 + x) * 2).astype(jnp.int32).reshape(1)

    route = routing[:, 0]
    other = lax.bitwise_xor(route, e)
    group = lax.bitwise_xor(other & 1, x) * 2 + (other >> 1)
    index = jnp.arange(local_rows, dtype=jnp.int32)
    earlier = (route[:, None] == route[None, :]) & (index[None, :] < index[:, None])
    slot = group * size + jnp.sum(earlier.astype(jnp.int32), axis=1)
    scale_lanes = jnp.broadcast_to(gate_scale[:, None], (local_rows, LANES))
    groups = pack(slot[None, :], token_rows, row_grads, scale_lanes, 4, size)

    def over_expert(a, g, cross=0):
        pairs = []
        for i in range(4):
            for j in range(2):
                d = (j ^ (g >> 1)) + 2 * (g & 1)
                pairs.append((i * 2 + j, (i ^ d) * 2 + (j ^ cross)))
        return lax.ppermute(a, ("expert", "etensor"), pairs)

    def along(a, pairs):
        return lax.ppermute(a, "dp", pairs)

    def across(a):
        return lax.ppermute(a, "etensor", ((0, 1), (1, 0)))

    near, far, near_other, far_other = (over_expert(a, g) for g, a in enumerate(groups))

    order = Order()
    flag = middle.astype(jnp.int32).reshape(1)
    weights = (w_gate, w_up, w_down)
    pair = 2 * size
    x_near = along(near, OUTER)
    middle_near = along(near, MIDDLE)
    xx_near = across(x_near)
    second_near = along(x_near, MIDDLE)
    out_near = along(middle_near, OUT)
    out_second = along(second_near, OUT)

    y_near, far_1 = choose(order, flag, [(middle_near, out_near)], [far])
    xy_near = across(y_near)
    ends_far = along(far_1, ENDS)
    in_far = along(far_1, IN_TWO)
    u1 = Unit(
        order,
        lane,
        flag,
        [near, near_other, far, far_other],
        [(0, pair, None), (pair, size, None), (pair + size, size, None)],
        weights,
    )
    z_near, far_2 = choose(order, flag, [(second_near, out_second)], [far])
    xz_near = across(z_near)
    middle_far = along(far_2, MIDDLE)
    out_far = along(far_2, OUT_TWO)
    x_far = along(far_2, OUTER)
    z_far, w_other = choose(order, flag, [(in_far, ends_far)], [u1.partials[2]])
    w_other = across(w_other)
    xz_far = across(z_far)
    u2 = Unit(
        order,
        lane,
        flag,
        [x_near, xx_near, y_near, xy_near, z_near, xz_near],
        [(0, pair, None), (pair, pair, None), (2 * pair, pair, None), (2 * pair, pair, pair)],
        weights,
    )
    y_far, x_far = choose(order, flag, [(middle_far, out_far)], [x_far], [xz_far, w_other])
    xy_far = across(y_far)
    xx_far = across(x_far)
    x_part, y_part, z_part, s_part = u2.partials
    near_terms = [
        along(x_part, OUTER),
        along(s_part, SKIP),
        along(y_part, MIDDLE),
        along(z_part, ENDS),
    ]
    u3 = Unit(
        order,
        lane,
        flag,
        [z_far, y_far, xz_far, xy_far],
        [(0, pair, None), (pair, pair, None)],
        weights,
    )
    zy_other = across(u3.partials[1])
    u4 = Unit(
        order, lane, flag, [x_far, xx_far], [(0, size, None), (size, size, None)], weights
    )
    x_other = across(u4.partials[1])
    terms = range(2, 7)
    z_part, y_part, s_part, near_own, near_other = sums(
        order,
        flag,
        [u3.partials[0], zy_other, u1.partials[0], *near_terms],
        [
            (size, [(0, 0), (1, 0)], None),
            (size, [(0, size), (1, size)], None),
            (size, [(0, 0), (1, 0)], [(0, size), (1, size)]),
            (size, [(k, 0) for k in terms], None),
            (size, [(k, size) for k in terms], None),
        ],
    )
    near_other = across(near_other)
    far_terms = [along(s_part, SKIP), along(y_part, MIDDLE), along(z_part, ENDS)]

    units_of = (u1, u2, u3, u4)
    rows = [piece for u in units_of for piece in u.pieces]
    scaled = [u.scaled for u in units_of]
    width = token_rows.shape[1]

    def grad_of(right, name):
        return weight_grad(order, right, [getattr(u, name) for u in units_of], width)

    grad_down = grad_of(scaled, "hidden")
    (x_part,) = sums(
        order, flag, [u4.partials[0], x_other], [(size, [(0, 0), (1, 0)], None)]
    )
    far_terms.append(along(x_part, OUTER))
    grad_gate = grad_of(rows, "gate_grad")
    near_own, far_own = sums(
        order,
        flag,
        [near_own, near_other, u1.partials[1], w_other, *far_terms],
        [(size, [(0, 0), (1, 0)], None), (size, [(k, 0) for k in range(2, 8)], None)],
    )
    far_back = [over_expert(far_own, 1), over_expert(far_own, 1, 1)]
    near_back = [over_expert(near_own, 0), over_expert(near_own, 0, 1)]
    grad_up = grad_of(rows, "up_grad")
    input_grads, scale_grads = unpack(
        order, slot[:, None], [near_back[0], far_back[0], near_back[1], far_back[1]], width
    )
    return (input_grads, scale_grads[:, 0], grad_gate[None], grad_up[None], grad_down[None])


def plain_device(token_rows, row_grads, gate_scale, routing, gate_weight, up_weight, down_weight):
    experts = lax.axis_size("expert")
    width = token_rows.shape[1]
    local_rows = token_rows.shape[0]
    capacity = 3 * local_rows // 8
    route = routing[:, 0]
    hits = (route[:, None] == jnp.arange(experts, dtype=jnp.int32)[None, :]).astype(jnp.int32)
    before = jnp.cumsum(hits, axis=0) - hits
    slot_pos = route * capacity + jnp.sum(before * hits, axis=1)
    placing = (
        jnp.arange(experts * capacity, dtype=jnp.int32)[:, None] == slot_pos[None, :]
    ).astype(jnp.bfloat16)
    send_rows = (
        jnp.dot(placing, token_rows, preferred_element_type=jnp.float32)
        .astype(jnp.bfloat16)
        .reshape(experts, capacity, width)
    )
    send_grads = (
        jnp.dot(placing, row_grads, preferred_element_type=jnp.float32)
        .astype(jnp.bfloat16)
        .reshape(experts, capacity, width)
    )
    send_scale = (
        jnp.dot(placing, gate_scale, preferred_element_type=jnp.float32)
        .astype(jnp.bfloat16)
        .reshape(experts, capacity)
    )
    recv_rows, recv_grads, recv_scale = (
        lax.all_to_all(send_rows, "expert", split_axis=0, concat_axis=0, tiled=True),
        lax.all_to_all(send_grads, "expert", split_axis=0, concat_axis=0, tiled=True),
        lax.all_to_all(send_scale, "expert", split_axis=0, concat_axis=0, tiled=True),
    )
    group_rows, group_grads, group_scale = (
        lax.all_gather(recv_rows.reshape(-1, width), "dp", axis=0, tiled=True),
        lax.all_gather(recv_grads.reshape(-1, width), "dp", axis=0, tiled=True),
        lax.all_gather(recv_scale.reshape(-1), "dp", axis=0, tiled=True),
    )
    w_gate = gate_weight[0]
    w_up = up_weight[0]
    w_down = down_weight[0]
    scale_column = group_scale.astype(jnp.float32)[:, None]
    gate_pre = jnp.einsum("rd,fd->rf", group_rows, w_gate, preferred_element_type=jnp.float32)
    up_pre = jnp.einsum("rd,fd->rf", group_rows, w_up, preferred_element_type=jnp.float32)
    sigmoid_gate = jax.nn.sigmoid(gate_pre)
    activated = gate_pre * sigmoid_gate
    hidden = (activated * up_pre).astype(jnp.bfloat16)
    hidden_raw = jnp.einsum("rd,fd->rf", group_grads, w_down, preferred_element_type=jnp.float32)
    scale_term = jnp.sum(hidden.astype(jnp.float32) * hidden_raw, axis=1)
    hidden_grad = scale_column * hidden_raw
    gate_pre_grad = (
        hidden_grad * up_pre * sigmoid_gate * (1.0 + gate_pre * (1.0 - sigmoid_gate))
    ).astype(jnp.bfloat16)
    up_pre_grad = (hidden_grad * activated).astype(jnp.bfloat16)
    scaled_grads = (scale_column * group_grads.astype(jnp.float32)).astype(jnp.bfloat16)
    grad_gate = jnp.einsum(
        "rf,rd->fd", gate_pre_grad, group_rows, preferred_element_type=jnp.float32
    ).astype(jnp.bfloat16)
    grad_up = jnp.einsum(
        "rf,rd->fd", up_pre_grad, group_rows, preferred_element_type=jnp.float32
    ).astype(jnp.bfloat16)
    grad_down = jnp.einsum(
        "rf,rd->fd", hidden, scaled_grads, preferred_element_type=jnp.float32
    ).astype(jnp.bfloat16)
    row_term = jnp.dot(gate_pre_grad, w_gate, preferred_element_type=jnp.float32) + jnp.dot(
        up_pre_grad, w_up, preferred_element_type=jnp.float32
    )
    share_total, share_scale = (
        lax.psum_scatter(row_term, ("dp", "etensor"), scatter_dimension=0, tiled=True),
        lax.psum_scatter(scale_term, ("dp", "etensor"), scatter_dimension=0, tiled=True),
    )
    row_total, scale_total = (
        lax.all_gather(share_total, "etensor", axis=0, tiled=True),
        lax.all_gather(share_scale, "etensor", axis=0, tiled=True),
    )
    back_rows, back_scale = (
        lax.all_to_all(
            row_total.reshape(experts, capacity, width),
            "expert",
            split_axis=0,
            concat_axis=0,
            tiled=True,
        ),
        lax.all_to_all(
            scale_total.reshape(experts, capacity),
            "expert",
            split_axis=0,
            concat_axis=0,
            tiled=True,
        ),
    )
    input_grads = jnp.take(back_rows.reshape(-1, width), slot_pos, axis=0).astype(jnp.bfloat16)
    scale_grads = jnp.take(back_scale.reshape(-1), slot_pos, axis=0)
    return (input_grads, scale_grads, grad_gate[None], grad_up[None], grad_down[None])


def solution(mesh):
    in_specs = (
        P(("dp", "expert"), None),
        P(("dp", "expert"), None),
        P(("dp", "expert")),
        P(("dp", "expert"), None),
        P("expert", ("dp", "etensor"), None),
        P("expert", ("dp", "etensor"), None),
        P("expert", ("dp", "etensor"), None),
    )
    out_specs = (
        P(("dp", "expert"), None),
        P(("dp", "expert")),
        P("expert", ("dp", "etensor"), None),
        P("expert", ("dp", "etensor"), None),
        P("expert", ("dp", "etensor"), None),
    )
    sizes = (mesh.shape["dp"], mesh.shape["expert"], mesh.shape["etensor"])
    per_device = line_device if sizes == (4, 4, 2) else plain_device
    return jax.shard_map(
        per_device, mesh=mesh, in_specs=in_specs, out_specs=out_specs, check_vma=False
    )
```

```python
import functools

import jax
import jax.numpy as jnp
from jax import lax
from jax.experimental import pallas as pl
from jax.experimental.pallas import tpu as pltpu
from jax.sharding import PartitionSpec as P

LANES = 128
F_BLOCK = 256
MIB = 1 << 20
VMEM = 56 * MIB
SMALL = pl.CostEstimate(flops=0, bytes_accessed=0, transcendentals=0)

PAIRS = [[(i, i ^ k) for i in range(4)] for k in range(4)]
MIDDLE = ((1, 2), (2, 1))
OUT = ((1, 0), (2, 3))


def nt_dot(a, b):
    return lax.dot_general(a, b, (((1,), (1,)), ((), ())), preferred_element_type=jnp.float32)


def tn_dot(a, b):
    return lax.dot_general(a, b, (((0,), (0,)), ((), ())), preferred_element_type=jnp.float32)


def pack_kernel(e_ref, x_ref, across_ref, down_ref, rows_in, grads_in, scale_ref, *refs):
    slot_out, out_refs = refs[0], refs[1:5]
    rows_ref, grads_ref, sems = refs[5:]
    width = rows_ref.shape[1]
    copies = [
        pltpu.make_async_copy(a, b, sems.at[i])
        for i, (a, b) in enumerate(((rows_in, rows_ref), (grads_in, grads_ref)))
    ]
    for copy in copies:
        copy.start()
    count = rows_ref.shape[0]
    size = out_refs[0].shape[0]
    route = across_ref[...]
    earlier = lax.broadcasted_iota(jnp.int32, (count, count), 0) < lax.broadcasted_iota(
        jnp.int32, (count, count), 1
    )
    same = (down_ref[...] == route) & earlier
    rank = jnp.sum(same.astype(jnp.int32), axis=0, keepdims=True)
    other = lax.bitwise_xor(route, e_ref[0])
    slot = (lax.bitwise_xor(other & 1, x_ref[0]) * 2 + (other >> 1)) * size + rank
    slot_out[...] = slot
    for copy in copies:
        copy.wait()
    for group, out_ref in enumerate(out_refs):
        at = lax.broadcasted_iota(jnp.int32, (size, count), 0) + group * size
        placing = (at == slot).astype(jnp.float32).astype(jnp.bfloat16)
        for start, ref in ((0, rows_ref), (width, grads_ref), (2 * width, scale_ref)):
            out_ref[:, start : start + ref.shape[1]] = jnp.dot(
                placing, ref[...], preferred_element_type=jnp.float32
            ).astype(jnp.bfloat16)


def pack(e, x, routing, rows, grads, scale, size):
    count, width = rows.shape
    scalar = pl.BlockSpec(memory_space=pltpu.SMEM)
    inside = pl.BlockSpec(memory_space=pltpu.VMEM)
    anywhere = pl.BlockSpec(memory_space=pl.ANY)
    return pl.pallas_call(
        pack_kernel,
        in_specs=[scalar, scalar, inside, inside, anywhere, anywhere, inside],
        out_specs=[inside] * 5,
        out_shape=[jax.ShapeDtypeStruct((1, count), jnp.int32)]
        + [jax.ShapeDtypeStruct((size, 2 * width + LANES), jnp.bfloat16)] * 4,
        scratch_shapes=[
            pltpu.VMEM((count, width), jnp.bfloat16),
            pltpu.VMEM((count, width), jnp.bfloat16),
            pltpu.SemaphoreType.DMA((2,)),
        ],
        compiler_params=pltpu.CompilerParams(vmem_limit_bytes=VMEM),
        cost_estimate=SMALL,
    )(e, x, routing.reshape(1, count), routing, rows, grads, scale)


def nothing_kernel(*refs):
    del refs


class Order:
    def __init__(self):
        self.token = jnp.zeros((8, LANES), jnp.float32)

    def call(self, kernel, operands, in_specs, out_shape, out_specs, **options):
        n_in, n_out = len(operands), len(out_shape)

        def body(*refs):
            ins, refs = refs[:n_in], refs[n_in + 1 :]
            outs, scratch = refs[:n_out], refs[n_out + 1 :]
            kernel(*ins, *outs, *scratch)

        anywhere = pl.BlockSpec(memory_space=pl.ANY)
        *out, self.token = pl.pallas_call(
            body,
            in_specs=[*in_specs, anywhere],
            out_specs=[*out_specs, anywhere],
            out_shape=[*out_shape, jax.ShapeDtypeStruct(self.token.shape, self.token.dtype)],
            input_output_aliases={n_in: n_out},
            compiler_params=pltpu.CompilerParams(vmem_limit_bytes=VMEM),
            cost_estimate=SMALL,
            **options,
        )(*operands, self.token)
        return out

    def wait(self, *arrays):
        self.call(nothing_kernel, arrays, [pl.BlockSpec(memory_space=pl.ANY)] * len(arrays), [], [])


def choose_kernel(picks, copies, needs, flag_ref, *refs):
    n_in = 2 * picks + copies
    ins, outs = refs[:n_in], refs[n_in + needs :]

    def move(first):
        for i in range(picks):
            outs[i][...] = ins[2 * i + 1 - first][...]

    pl.when(flag_ref[0] == 1)(functools.partial(move, 1))
    pl.when(flag_ref[0] != 1)(functools.partial(move, 0))
    for i in range(copies):
        outs[picks + i][...] = ins[2 * picks + i][...]


def choose(order, flag, pairs, singles=(), needs=()):
    moved = [*[a for pair in pairs for a in pair], *singles]
    inside = pl.BlockSpec(memory_space=pltpu.VMEM)
    out_shape = [jax.ShapeDtypeStruct(a.shape, a.dtype) for a in [p[0] for p in pairs] + list(singles)]
    return order.call(
        functools.partial(choose_kernel, len(pairs), len(singles), len(needs)),
        [flag, *moved, *needs],
        [pl.BlockSpec(memory_space=pltpu.SMEM)]
        + [inside] * len(moved)
        + [pl.BlockSpec(memory_space=pl.ANY)] * len(needs),
        out_shape,
        [inside] * len(out_shape),
    )


def sum_kernel(plan, size, *refs):
    for pieces, out_ref in zip(plan, refs[len(refs) - len(plan) :], strict=True):
        for i, terms in enumerate(pieces):
            total = None
            for k, start in terms:
                term = refs[k][start : start + size, :].astype(jnp.float32)
                total = term if total is None else total + term
            out_ref[i * size : (i + 1) * size, :] = total.astype(out_ref.dtype)


def sums(order, operands, size, *plan):
    width = operands[0].shape[1]
    inside = pl.BlockSpec(memory_space=pltpu.VMEM)
    return order.call(
        functools.partial(sum_kernel, plan, size),
        operands,
        [inside] * len(operands),
        [jax.ShapeDtypeStruct((size * len(pieces), width), jnp.bfloat16) for pieces in plan],
        [inside] * len(plan),
    )


def unit_kernel(n_pieces, parts, count, lane_ref, *refs):
    pieces = refs[:n_pieces]
    weights = refs[n_pieces : n_pieces + 3]
    refs = refs[n_pieces + 3 :]
    outs, scaled_out = refs[:3], refs[3]
    partial_refs = refs[4 : 4 + len(parts)]
    (
        rows_ref,
        grads_ref,
        scale_ref,
        scaled_ref,
        total_ref,
        scale_sum_ref,
        held_ref,
        act_ref,
        piece_sems,
        weight_sems,
        act_sems,
        scaled_sem,
    ) = refs[4 + len(parts) :]
    size = pieces[0].shape[0]
    width = rows_ref.shape[1]
    slots = held_ref.shape[0]

    def weight_copy(i, k):
        return pltpu.make_async_copy(
            weights[k].at[pl.ds(i * F_BLOCK, F_BLOCK), :],
            held_ref.at[lax.rem(i, slots), k],
            weight_sems.at[lax.rem(i, slots), k],
        )

    def act_copy(i, k):
        return pltpu.make_async_copy(
            act_ref.at[lax.rem(i, 2), k],
            outs[k].at[:, pl.ds(pl.multiple_of(i * F_BLOCK, F_BLOCK), F_BLOCK)],
            act_sems.at[lax.rem(i, 2), k],
        )

    def piece_copies(j, start, ref):
        return [
            pltpu.make_async_copy(
                piece.at[:, pl.ds(start, ref.shape[1])],
                ref.at[pl.ds(i * size, size), :],
                piece_sems.at[i, j],
            )
            for i, piece in enumerate(pieces)
        ]

    row_copies = piece_copies(0, 0, rows_ref)
    grad_copies = piece_copies(1, width, grads_ref) + piece_copies(2, 2 * width, scale_ref)
    for copy in row_copies:
        copy.start()
    weight_copy(0, 0).start()
    weight_copy(0, 1).start()
    for copy in grad_copies:
        copy.start()
    weight_copy(0, 2).start()
    for k in range(3):
        weight_copy(1, k).start()
    total_ref[...] = jnp.zeros_like(total_ref)
    scale_sum_ref[...] = jnp.zeros_like(scale_sum_ref)
    for copy in row_copies + grad_copies:
        copy.wait()
    scale = scale_ref[:, 0:1].astype(jnp.float32)
    scaled_ref[...] = (scale * grads_ref[...].astype(jnp.float32)).astype(jnp.bfloat16)
    scaled_copy = pltpu.make_async_copy(scaled_ref, scaled_out, scaled_sem)
    scaled_copy.start()

    def products(i):
        held = held_ref.at[lax.rem(i, slots)]
        gate_pre = nt_dot(rows_ref[...], held[0])
        up_pre = nt_dot(rows_ref[...], held[1])
        raw = nt_dot(grads_ref[...], held[2])
        return gate_pre, up_pre, raw

    def activate(i, gate_pre, up_pre, raw):
        sigmoid = jax.nn.sigmoid(gate_pre)
        activated = gate_pre * sigmoid
        hidden = (activated * up_pre).astype(jnp.bfloat16)
        scale_sum_ref[...] += jnp.sum(hidden.astype(jnp.float32) * raw, axis=1, keepdims=True)
        hidden_grad = scale_ref[:, 0:1].astype(jnp.float32) * raw
        act = act_ref.at[lax.rem(i, 2)]
        act[0] = hidden
        act[1] = (
            hidden_grad * up_pre * sigmoid * (1.0 + gate_pre * (1.0 - sigmoid))
        ).astype(jnp.bfloat16)
        act[2] = (hidden_grad * activated).astype(jnp.bfloat16)

    def add_inputs(i, finish=None):
        held = held_ref.at[lax.rem(i, slots)]
        act = act_ref.at[lax.rem(i, 2)]
        gate_grad, up_grad = act[1], act[2]
        tile = 1024
        for start in range(0, width, tile):
            at = slice(start, start + tile)
            total = (
                total_ref[:, at]
                + jnp.dot(gate_grad, held[0, :, at], preferred_element_type=jnp.float32)
                + jnp.dot(up_grad, held[1, :, at], preferred_element_type=jnp.float32)
            )
            if finish is None:
                total_ref[:, at] = total
            else:
                finish(at, total)

    def arrive(i):
        for k in range(3):
            weight_copy(i, k).wait()

        @pl.when(i + 2 < count)
        def _():
            for k in range(3):
                weight_copy(i + 2, k).start()

    arrive(0)
    activate(0, *products(0))
    for k in range(3):
        act_copy(0, k).start()

    def step(i, carry):
        arrive(i)

        @pl.when(i >= 2)
        def _():
            for k in range(3):
                act_copy(i - 2, k).wait()

        now = products(i)
        add_inputs(i - 1)
        activate(i, *now)
        for k in range(3):
            act_copy(i, k).start()
        return carry

    lax.fori_loop(1, count, step, 0)

    def write(at, value):
        start = 0
        for ref, size in zip(partial_refs, parts, strict=True):
            ref[:, at] = value[start : start + size].astype(jnp.bfloat16)
            start += size

    add_inputs(count - 1, write)
    value = scale_sum_ref[...]
    high = value.astype(jnp.bfloat16).astype(jnp.float32)
    lane = lax.broadcasted_iota(jnp.int32, (value.shape[0], LANES), 1)
    first = lane_ref[0]
    lanes = jnp.where(lane == first, high, jnp.where(lane == first + 1, value - high, 0.0))
    write(slice(width, width + LANES), lanes)
    for i in (count - 2, count - 1):
        for k in range(3):
            act_copy(i, k).wait()
    scaled_copy.wait()


class Unit:
    def __init__(self, order, lane, pieces, parts, weights):
        size = pieces[0].shape[0]
        rows = size * len(pieces)
        units, width = weights[0].shape
        count = units // F_BLOCK
        anywhere = pl.BlockSpec(memory_space=pl.ANY)
        inside = pl.BlockSpec(memory_space=pltpu.VMEM)
        scalar = pl.BlockSpec(memory_space=pltpu.SMEM)
        bf16 = jnp.bfloat16
        out = order.call(
            functools.partial(unit_kernel, len(pieces), parts, count),
            [lane, *pieces, *weights],
            [scalar] + [anywhere] * (len(pieces) + 3),
            [jax.ShapeDtypeStruct((rows, units), bf16)] * 3
            + [jax.ShapeDtypeStruct((rows, width), bf16)]
            + [jax.ShapeDtypeStruct((part, width + LANES), bf16) for part in parts],
            [anywhere] * 4 + [inside] * len(parts),
            scratch_shapes=[
                pltpu.VMEM((rows, width), bf16),
                pltpu.VMEM((rows, width), bf16),
                pltpu.VMEM((rows, LANES), bf16),
                pltpu.VMEM((rows, width), bf16),
                pltpu.VMEM((rows, width), jnp.float32),
                pltpu.VMEM((rows, 1), jnp.float32),
                pltpu.VMEM((4, 3, F_BLOCK, width), bf16),
                pltpu.VMEM((2, 3, rows, F_BLOCK), bf16),
                pltpu.SemaphoreType.DMA((len(pieces), 3)),
                pltpu.SemaphoreType.DMA((4, 3)),
                pltpu.SemaphoreType.DMA((2, 3)),
                pltpu.SemaphoreType.DMA(()),
            ],
        )
        self.hidden, self.gate_grad, self.up_grad, self.scaled = out[:4]
        self.partials = out[4:]
        self.pieces = pieces


def weight_kernel(n_right, n_left, n_out, *refs):
    right, refs = refs[:n_right], refs[n_right:]
    left, refs = refs[: n_left * n_out], refs[n_left * n_out :]
    out_refs, (rows_ref, sems) = refs[:n_out], refs[n_out:]
    width = rows_ref.shape[1]

    @pl.when(pl.program_id(0) == 0)
    def _():
        copies, start = [], 0
        for i, ref in enumerate(right):
            size = ref.shape[0]
            copies.append(
                pltpu.make_async_copy(
                    ref.at[:, pl.ds(0, width)], rows_ref.at[pl.ds(start, size), :], sems.at[i]
                )
            )
            start += size
        for copy in copies:
            copy.start()
        for copy in copies:
            copy.wait()

    tile = 1024
    for k, out_ref in enumerate(out_refs):
        both = jnp.concatenate([ref[...] for ref in left[k * n_left : (k + 1) * n_left]], axis=0)
        for start in range(0, width, tile):
            at = slice(start, start + tile)
            out_ref[:, at] = tn_dot(both, rows_ref[:, at]).astype(jnp.bfloat16)


def weight_grads(order, right, lefts, width):
    left = [a for one in lefts for a in one]
    rows = sum(a.shape[0] for a in lefts[0])
    units = left[0].shape[1]
    anywhere = pl.BlockSpec(memory_space=pl.ANY)
    return order.call(
        functools.partial(weight_kernel, len(right), len(lefts[0]), len(lefts)),
        [*right, *left],
        [anywhere] * len(right)
        + [pl.BlockSpec((a.shape[0], F_BLOCK), lambda i: (0, i)) for a in left],
        [jax.ShapeDtypeStruct((units, width), jnp.bfloat16)] * len(lefts),
        [pl.BlockSpec((F_BLOCK, width), lambda i: (i, 0))] * len(lefts),
        grid=(units // F_BLOCK,),
        scratch_shapes=[
            pltpu.VMEM((rows, width), jnp.bfloat16),
            pltpu.SemaphoreType.DMA((len(right),)),
        ],
    )


def unpack_kernel(slot_ref, *refs):
    grads_ref, scale_ref = refs[-2:]
    width = grads_ref.shape[1]
    slot = slot_ref[...]
    total = jnp.zeros((slot.shape[0], width + LANES), jnp.float32)
    for group, ref in enumerate(refs[:-2]):
        size = ref.shape[0]
        at = lax.broadcasted_iota(jnp.int32, (slot.shape[0], size), 1) + group * size
        placing = (at == slot).astype(jnp.float32).astype(jnp.bfloat16)
        total += jnp.dot(placing, ref[...], preferred_element_type=jnp.float32)
    grads_ref[...] = total[:, :width].astype(jnp.bfloat16)
    ones = jnp.ones((8, LANES), jnp.bfloat16)
    scale_ref[...] = nt_dot(ones, total[:, width:].astype(jnp.bfloat16))[0:1, :]


def unpack(order, slot, groups, width):
    rows = slot.shape[0]
    inside = pl.BlockSpec(memory_space=pltpu.VMEM)
    return order.call(
        unpack_kernel,
        [slot, *groups],
        [inside] * (1 + len(groups)),
        [
            jax.ShapeDtypeStruct((rows, width), jnp.bfloat16),
            jax.ShapeDtypeStruct((1, rows), jnp.float32),
        ],
        [inside] * 2,
    )


def line_device(token_rows, row_grads, gate_scale, routing, gate_weight, up_weight, down_weight):
    width = token_rows.shape[1]
    local_rows = token_rows.shape[0]
    size = 3 * local_rows // 8
    z, e, x = (lax.axis_index(name) for name in ("dp", "expert", "etensor"))
    middle = (z == 1) | (z == 2)
    w_gate, w_up, w_down = gate_weight[0], up_weight[0], down_weight[0]
    lane = ((z * 2 + x) * 2).astype(jnp.int32).reshape(1)

    scale_lanes = jnp.broadcast_to(gate_scale[:, None], (local_rows, LANES))
    slot, *groups = pack(
        e.astype(jnp.int32).reshape(1),
        x.astype(jnp.int32).reshape(1),
        routing,
        token_rows,
        row_grads,
        scale_lanes,
        size,
    )

    def over_expert(a, g, cross=0):
        pairs = []
        for i in range(4):
            for j in range(2):
                d = (j ^ (g >> 1)) + 2 * (g & 1)
                pairs.append((i * 2 + j, (i ^ d) * 2 + (j ^ cross)))
        return lax.ppermute(a, ("expert", "etensor"), pairs)

    def along(a, pairs):
        return lax.ppermute(a, "dp", pairs)

    def across(a):
        return lax.ppermute(a, "etensor", ((0, 1), (1, 0)))

    near, far, near_other, far_other = (over_expert(a, g) for g, a in enumerate(groups))

    order = Order()
    flag = middle.astype(jnp.int32).reshape(1)
    weights = (w_gate, w_up, w_down)
    pair = 2 * size
    near_1 = along(near, PAIRS[1])
    middle_near = along(near, MIDDLE)
    order.wait(near_1, middle_near, near_other, far)
    second_near = along(near_1, MIDDLE)
    out_near = along(middle_near, OUT)
    swap_1 = across(near_1)
    (near_2,) = choose(order, flag, [(second_near, out_near)])
    out_second = along(second_near, OUT)
    swap_2 = across(near_2)
    near_3, far_copy = choose(order, flag, [(middle_near, out_second)], [far], [swap_1, far_other])
    swap_3 = across(near_3)
    far_3 = along(far_copy, PAIRS[3])
    far_1 = along(far_copy, PAIRS[1])
    u0 = Unit(order, lane, [near, near_other, far, far_other], [pair, size, size], weights)
    far_3, far_1, far_copy = choose(order, flag, [], [far_3, far_1, far], [swap_2])
    far_swap_3 = across(far_3)
    far_swap_1 = across(far_1)
    far_2 = along(far_copy, PAIRS[2])
    u1 = Unit(
        order, lane, [near_1, swap_1, near_2, swap_2, near_3, swap_3], [pair, pair, pair], weights
    )
    (far_2,) = choose(order, flag, [], [far_2], [far_swap_3])
    far_swap_2 = across(far_2)
    near_terms = [along(a, PAIRS[k + 1]) for k, a in enumerate(u1.partials)]
    u2 = Unit(order, lane, [far_3, far_1, far_swap_3, far_swap_1], [pair, pair], weights)
    others = across(u2.partials[1])
    order.wait(near_terms[0], near_terms[2])
    u3 = Unit(order, lane, [far_2, far_swap_2], [size, size], weights)
    other_2 = across(u3.partials[1])
    part_3, part_1 = sums(
        order, [u2.partials[0], others], size, [[(0, 0), (1, 0)]], [[(0, size), (1, size)]]
    )
    far_terms = [along(part_3, PAIRS[3]), along(part_1, PAIRS[1])]
    (part_2,) = sums(order, [u3.partials[0], other_2], size, [[(0, 0), (1, 0)]])
    far_terms.append(along(part_2, PAIRS[2]))
    terms = range(4)
    near_own, rest = sums(
        order,
        [u0.partials[0], *near_terms, u0.partials[2]],
        size,
        [[(k, 0) for k in terms]],
        [[(k, size) for k in terms], [(4, 0)]],
    )
    rest = across(rest)

    units_of = (u0, u1, u2, u3)
    rows = [piece for u in units_of for piece in u.pieces]
    scaled = [u.scaled for u in units_of]
    width = token_rows.shape[1]

    def grads_of(right, *names):
        lefts = [[getattr(u, name) for u in units_of] for name in names]
        return weight_grads(order, right, lefts, width)

    grad_gate, grad_up = grads_of(rows, "gate_grad", "up_grad")
    near_own, far_own = sums(
        order,
        [near_own, rest, u0.partials[1], *far_terms],
        size,
        [[(0, 0), (1, 0)]],
        [[(1, size), *[(k, 0) for k in range(2, 6)]]],
    )
    far_back = [over_expert(far_own, 1), over_expert(far_own, 1, 1)]
    near_back = [over_expert(near_own, 0), over_expert(near_own, 0, 1)]
    (grad_down,) = grads_of(scaled, "hidden")
    input_grads, scale_grads = unpack(
        order, slot.reshape(-1, 1), [near_back[0], far_back[0], near_back[1], far_back[1]], width
    )
    return (input_grads, scale_grads[0], grad_gate[None], grad_up[None], grad_down[None])


def plain_device(token_rows, row_grads, gate_scale, routing, gate_weight, up_weight, down_weight):
    experts = lax.axis_size("expert")
    width = token_rows.shape[1]
    local_rows = token_rows.shape[0]
    capacity = 3 * local_rows // 8
    route = routing[:, 0]
    hits = (route[:, None] == jnp.arange(experts, dtype=jnp.int32)[None, :]).astype(jnp.int32)
    before = jnp.cumsum(hits, axis=0) - hits
    slot_pos = route * capacity + jnp.sum(before * hits, axis=1)
    placing = (
        jnp.arange(experts * capacity, dtype=jnp.int32)[:, None] == slot_pos[None, :]
    ).astype(jnp.bfloat16)
    send_rows = (
        jnp.dot(placing, token_rows, preferred_element_type=jnp.float32)
        .astype(jnp.bfloat16)
        .reshape(experts, capacity, width)
    )
    send_grads = (
        jnp.dot(placing, row_grads, preferred_element_type=jnp.float32)
        .astype(jnp.bfloat16)
        .reshape(experts, capacity, width)
    )
    send_scale = (
        jnp.dot(placing, gate_scale, preferred_element_type=jnp.float32)
        .astype(jnp.bfloat16)
        .reshape(experts, capacity)
    )
    recv_rows, recv_grads, recv_scale = (
        lax.all_to_all(send_rows, "expert", split_axis=0, concat_axis=0, tiled=True),
        lax.all_to_all(send_grads, "expert", split_axis=0, concat_axis=0, tiled=True),
        lax.all_to_all(send_scale, "expert", split_axis=0, concat_axis=0, tiled=True),
    )
    group_rows, group_grads, group_scale = (
        lax.all_gather(recv_rows.reshape(-1, width), "dp", axis=0, tiled=True),
        lax.all_gather(recv_grads.reshape(-1, width), "dp", axis=0, tiled=True),
        lax.all_gather(recv_scale.reshape(-1), "dp", axis=0, tiled=True),
    )
    w_gate = gate_weight[0]
    w_up = up_weight[0]
    w_down = down_weight[0]
    scale_column = group_scale.astype(jnp.float32)[:, None]
    gate_pre = jnp.einsum("rd,fd->rf", group_rows, w_gate, preferred_element_type=jnp.float32)
    up_pre = jnp.einsum("rd,fd->rf", group_rows, w_up, preferred_element_type=jnp.float32)
    sigmoid_gate = jax.nn.sigmoid(gate_pre)
    activated = gate_pre * sigmoid_gate
    hidden = (activated * up_pre).astype(jnp.bfloat16)
    hidden_raw = jnp.einsum("rd,fd->rf", group_grads, w_down, preferred_element_type=jnp.float32)
    scale_term = jnp.sum(hidden.astype(jnp.float32) * hidden_raw, axis=1)
    hidden_grad = scale_column * hidden_raw
    gate_pre_grad = (
        hidden_grad * up_pre * sigmoid_gate * (1.0 + gate_pre * (1.0 - sigmoid_gate))
    ).astype(jnp.bfloat16)
    up_pre_grad = (hidden_grad * activated).astype(jnp.bfloat16)
    scaled_grads = (scale_column * group_grads.astype(jnp.float32)).astype(jnp.bfloat16)
    grad_gate = jnp.einsum(
        "rf,rd->fd", gate_pre_grad, group_rows, preferred_element_type=jnp.float32
    ).astype(jnp.bfloat16)
    grad_up = jnp.einsum(
        "rf,rd->fd", up_pre_grad, group_rows, preferred_element_type=jnp.float32
    ).astype(jnp.bfloat16)
    grad_down = jnp.einsum(
        "rf,rd->fd", hidden, scaled_grads, preferred_element_type=jnp.float32
    ).astype(jnp.bfloat16)
    row_term = jnp.dot(gate_pre_grad, w_gate, preferred_element_type=jnp.float32) + jnp.dot(
        up_pre_grad, w_up, preferred_element_type=jnp.float32
    )
    share_total, share_scale = (
        lax.psum_scatter(row_term, ("dp", "etensor"), scatter_dimension=0, tiled=True),
        lax.psum_scatter(scale_term, ("dp", "etensor"), scatter_dimension=0, tiled=True),
    )
    row_total, scale_total = (
        lax.all_gather(share_total, "etensor", axis=0, tiled=True),
        lax.all_gather(share_scale, "etensor", axis=0, tiled=True),
    )
    back_rows, back_scale = (
        lax.all_to_all(
            row_total.reshape(experts, capacity, width),
            "expert",
            split_axis=0,
            concat_axis=0,
            tiled=True,
        ),
        lax.all_to_all(
            scale_total.reshape(experts, capacity),
            "expert",
            split_axis=0,
            concat_axis=0,
            tiled=True,
        ),
    )
    input_grads = jnp.take(back_rows.reshape(-1, width), slot_pos, axis=0).astype(jnp.bfloat16)
    scale_grads = jnp.take(back_scale.reshape(-1), slot_pos, axis=0)
    return (input_grads, scale_grads, grad_gate[None], grad_up[None], grad_down[None])


def solution(mesh):
    in_specs = (
        P(("dp", "expert"), None),
        P(("dp", "expert"), None),
        P(("dp", "expert")),
        P(("dp", "expert"), None),
        P("expert", ("dp", "etensor"), None),
        P("expert", ("dp", "etensor"), None),
        P("expert", ("dp", "etensor"), None),
    )
    out_specs = (
        P(("dp", "expert"), None),
        P(("dp", "expert")),
        P("expert", ("dp", "etensor"), None),
        P("expert", ("dp", "etensor"), None),
        P("expert", ("dp", "etensor"), None),
    )
    sizes = (mesh.shape["dp"], mesh.shape["expert"], mesh.shape["etensor"])
    per_device = line_device if sizes == (4, 4, 2) else plain_device
    return jax.shard_map(
        per_device, mesh=mesh, in_specs=in_specs, out_specs=out_specs, check_vma=False
    )
```

```python
import functools

import jax
import jax.numpy as jnp
from jax import lax
from jax.experimental import pallas as pl
from jax.experimental.pallas import tpu as pltpu
from jax.sharding import PartitionSpec as P

LANES = 128
F_BLOCK = 256
MIB = 1 << 20
VMEM = 56 * MIB
SMALL = pl.CostEstimate(flops=0, bytes_accessed=0, transcendentals=0)

PAIRS = [[(i, i ^ k) for i in range(4)] for k in range(4)]
MIDDLE = ((1, 2), (2, 1))
OUT = ((1, 0), (2, 3))


def nt_dot(a, b):
    return lax.dot_general(a, b, (((1,), (1,)), ((), ())), preferred_element_type=jnp.float32)


def tn_dot(a, b):
    return lax.dot_general(a, b, (((0,), (0,)), ((), ())), preferred_element_type=jnp.float32)


def as_column(row):
    count = row.shape[1]
    diagonal = lax.broadcasted_iota(jnp.int32, (count, count), 0) == lax.broadcasted_iota(
        jnp.int32, (count, count), 1
    )
    return jnp.sum(jnp.where(diagonal, row, 0), axis=1, keepdims=True)


def pack_kernel(e_ref, x_ref, route_ref, scale_ref, rows_in, grads_in, *refs):
    slot_out, out_refs = refs[0], refs[1:5]
    rows_ref, grads_ref, sems = refs[5:]
    width = rows_ref.shape[1]
    copies = [
        pltpu.make_async_copy(a, b, sems.at[i])
        for i, (a, b) in enumerate(((rows_in, rows_ref), (grads_in, grads_ref)))
    ]
    for copy in copies:
        copy.start()
    count = rows_ref.shape[0]
    size = out_refs[0].shape[0]
    route = route_ref[...]
    earlier = lax.broadcasted_iota(jnp.int32, (count, count), 0) < lax.broadcasted_iota(
        jnp.int32, (count, count), 1
    )
    same = (as_column(route) == route) & earlier
    rank = jnp.sum(same.astype(jnp.int32), axis=0, keepdims=True)
    other = lax.bitwise_xor(route, e_ref[0])
    slot = (lax.bitwise_xor(other & 1, x_ref[0]) * 2 + (other >> 1)) * size + rank
    slot_out[...] = slot
    scale = scale_ref[...].astype(jnp.float32)
    placings = []
    for group, out_ref in enumerate(out_refs):
        at = lax.broadcasted_iota(jnp.int32, (size, count), 0) + group * size
        placing = (at == slot).astype(jnp.float32)
        placings.append(placing.astype(jnp.bfloat16))
        placed = jnp.sum(placing * scale, axis=1, keepdims=True)
        out_ref[:, 2 * width :] = jnp.broadcast_to(placed, (size, LANES)).astype(jnp.bfloat16)
    for copy in copies:
        copy.wait()
    for placing, out_ref in zip(placings, out_refs, strict=True):
        for start, ref in ((0, rows_ref), (width, grads_ref)):
            out_ref[:, start : start + width] = jnp.dot(
                placing, ref[...], preferred_element_type=jnp.float32
            ).astype(jnp.bfloat16)


def pack(e, x, route, scale, rows, grads, size):
    count, width = rows.shape
    scalar = pl.BlockSpec(memory_space=pltpu.SMEM)
    inside = pl.BlockSpec(memory_space=pltpu.VMEM)
    anywhere = pl.BlockSpec(memory_space=pl.ANY)
    return pl.pallas_call(
        pack_kernel,
        in_specs=[scalar, scalar, inside, inside, anywhere, anywhere],
        out_specs=[inside] * 5,
        out_shape=[jax.ShapeDtypeStruct((1, count), jnp.int32)]
        + [jax.ShapeDtypeStruct((size, 2 * width + LANES), jnp.bfloat16)] * 4,
        scratch_shapes=[
            pltpu.VMEM((count, width), jnp.bfloat16),
            pltpu.VMEM((count, width), jnp.bfloat16),
            pltpu.SemaphoreType.DMA((2,)),
        ],
        compiler_params=pltpu.CompilerParams(vmem_limit_bytes=VMEM),
        cost_estimate=SMALL,
    )(e, x, route, scale, rows, grads)


def nothing_kernel(*refs):
    del refs


class Order:
    def __init__(self):
        self.token = jnp.zeros((8, LANES), jnp.float32)

    def call(self, kernel, operands, in_specs, out_shape, out_specs, **options):
        n_in, n_out = len(operands), len(out_shape)

        def body(*refs):
            ins, refs = refs[:n_in], refs[n_in + 1 :]
            outs, scratch = refs[:n_out], refs[n_out + 1 :]
            kernel(*ins, *outs, *scratch)

        anywhere = pl.BlockSpec(memory_space=pl.ANY)
        *out, self.token = pl.pallas_call(
            body,
            in_specs=[*in_specs, anywhere],
            out_specs=[*out_specs, anywhere],
            out_shape=[*out_shape, jax.ShapeDtypeStruct(self.token.shape, self.token.dtype)],
            input_output_aliases={n_in: n_out},
            compiler_params=pltpu.CompilerParams(vmem_limit_bytes=VMEM),
            cost_estimate=SMALL,
            **options,
        )(*operands, self.token)
        return out

    def wait(self, *arrays):
        self.call(nothing_kernel, arrays, [pl.BlockSpec(memory_space=pl.ANY)] * len(arrays), [], [])


def choose_kernel(picks, copies, needs, flag_ref, *refs):
    n_in = 2 * picks + copies
    ins, outs = refs[:n_in], refs[n_in + needs :]

    def move(first):
        for i in range(picks):
            outs[i][...] = ins[2 * i + 1 - first][...]

    pl.when(flag_ref[0] == 1)(functools.partial(move, 1))
    pl.when(flag_ref[0] != 1)(functools.partial(move, 0))
    for i in range(copies):
        outs[picks + i][...] = ins[2 * picks + i][...]


def choose(order, flag, pairs, singles=(), needs=()):
    moved = [*[a for pair in pairs for a in pair], *singles]
    inside = pl.BlockSpec(memory_space=pltpu.VMEM)
    out_shape = [jax.ShapeDtypeStruct(a.shape, a.dtype) for a in [p[0] for p in pairs] + list(singles)]
    return order.call(
        functools.partial(choose_kernel, len(pairs), len(singles), len(needs)),
        [flag, *moved, *needs],
        [pl.BlockSpec(memory_space=pltpu.SMEM)]
        + [inside] * len(moved)
        + [pl.BlockSpec(memory_space=pl.ANY)] * len(needs),
        out_shape,
        [inside] * len(out_shape),
    )


def sum_kernel(plan, size, *refs):
    for pieces, out_ref in zip(plan, refs[len(refs) - len(plan) :], strict=True):
        for i, terms in enumerate(pieces):
            total = None
            for k, start in terms:
                term = refs[k][start : start + size, :].astype(jnp.float32)
                total = term if total is None else total + term
            out_ref[i * size : (i + 1) * size, :] = total.astype(out_ref.dtype)


def sums(order, operands, size, *plan):
    width = operands[0].shape[1]
    inside = pl.BlockSpec(memory_space=pltpu.VMEM)
    return order.call(
        functools.partial(sum_kernel, plan, size),
        operands,
        [inside] * len(operands),
        [jax.ShapeDtypeStruct((size * len(pieces), width), jnp.bfloat16) for pieces in plan],
        [inside] * len(plan),
    )


def unit_kernel(n_pieces, parts, count, lane_ref, *refs):
    pieces = refs[:n_pieces]
    weights = refs[n_pieces : n_pieces + 3]
    refs = refs[n_pieces + 3 :]
    outs, scaled_out = refs[:3], refs[3]
    partial_refs = refs[4 : 4 + len(parts)]
    (
        rows_ref,
        grads_ref,
        scale_ref,
        scaled_ref,
        total_ref,
        scale_sum_ref,
        held_ref,
        act_ref,
        piece_sems,
        weight_sems,
        act_sems,
        scaled_sem,
    ) = refs[4 + len(parts) :]
    size = pieces[0].shape[0]
    width = rows_ref.shape[1]
    slots = held_ref.shape[0]

    def weight_copy(i, k):
        return pltpu.make_async_copy(
            weights[k].at[pl.ds(i * F_BLOCK, F_BLOCK), :],
            held_ref.at[lax.rem(i, slots), k],
            weight_sems.at[lax.rem(i, slots), k],
        )

    def act_copy(i, k):
        return pltpu.make_async_copy(
            act_ref.at[lax.rem(i, 2), k],
            outs[k].at[:, pl.ds(pl.multiple_of(i * F_BLOCK, F_BLOCK), F_BLOCK)],
            act_sems.at[lax.rem(i, 2), k],
        )

    def piece_copies(j, start, ref):
        return [
            pltpu.make_async_copy(
                piece.at[:, pl.ds(start, ref.shape[1])],
                ref.at[pl.ds(i * size, size), :],
                piece_sems.at[i, j],
            )
            for i, piece in enumerate(pieces)
        ]

    row_copies = piece_copies(0, 0, rows_ref)
    grad_copies = piece_copies(1, width, grads_ref) + piece_copies(2, 2 * width, scale_ref)
    for copy in row_copies:
        copy.start()
    weight_copy(0, 0).start()
    weight_copy(0, 1).start()
    for copy in grad_copies:
        copy.start()
    weight_copy(0, 2).start()
    for k in range(3):
        weight_copy(1, k).start()
    scale_sum_ref[...] = jnp.zeros_like(scale_sum_ref)
    for copy in row_copies + grad_copies:
        copy.wait()
    scaled_copy = pltpu.make_async_copy(scaled_ref, scaled_out, scaled_sem)

    def products(i):
        held = held_ref.at[lax.rem(i, slots)]
        gate_pre = nt_dot(rows_ref[...], held[0])
        up_pre = nt_dot(rows_ref[...], held[1])
        raw = nt_dot(grads_ref[...], held[2])
        return gate_pre, up_pre, raw

    def activate(i, gate_pre, up_pre, raw):
        sigmoid = jax.nn.sigmoid(gate_pre)
        activated = gate_pre * sigmoid
        hidden = (activated * up_pre).astype(jnp.bfloat16)
        scale_sum_ref[...] += jnp.sum(hidden.astype(jnp.float32) * raw, axis=1, keepdims=True)
        hidden_grad = scale_ref[:, 0:1].astype(jnp.float32) * raw
        act = act_ref.at[lax.rem(i, 2)]
        act[0] = hidden
        act[1] = (
            hidden_grad * up_pre * sigmoid * (1.0 + gate_pre * (1.0 - sigmoid))
        ).astype(jnp.bfloat16)
        act[2] = (hidden_grad * activated).astype(jnp.bfloat16)

    def add_inputs(i, finish=None):
        held = held_ref.at[lax.rem(i, slots)]
        act = act_ref.at[lax.rem(i, 2)]
        gate_grad, up_grad = act[1], act[2]
        tile = 1024
        for start in range(0, width, tile):
            at = slice(start, start + tile)
            total = (
                total_ref[:, at]
                + jnp.dot(gate_grad, held[0, :, at], preferred_element_type=jnp.float32)
                + jnp.dot(up_grad, held[1, :, at], preferred_element_type=jnp.float32)
            )
            if finish is None:
                total_ref[:, at] = total
            else:
                finish(at, total)

    def arrive(i):
        for k in range(3):
            weight_copy(i, k).wait()

        @pl.when(i + 2 < count)
        def _():
            for k in range(3):
                weight_copy(i + 2, k).start()

    arrive(0)
    first_products = products(0)
    total_ref[...] = jnp.zeros_like(total_ref)
    scale = scale_ref[:, 0:1].astype(jnp.float32)
    scaled_ref[...] = (scale * grads_ref[...].astype(jnp.float32)).astype(jnp.bfloat16)
    activate(0, *first_products)
    scaled_copy.start()
    for k in range(3):
        act_copy(0, k).start()

    def step(i, carry):
        arrive(i)

        @pl.when(i >= 2)
        def _():
            for k in range(3):
                act_copy(i - 2, k).wait()

        now = products(i)
        add_inputs(i - 1)
        activate(i, *now)
        for k in range(3):
            act_copy(i, k).start()
        return carry

    lax.fori_loop(1, count, step, 0)

    def write(at, value):
        start = 0
        for ref, size in zip(partial_refs, parts, strict=True):
            ref[:, at] = value[start : start + size].astype(jnp.bfloat16)
            start += size

    add_inputs(count - 1, write)
    value = scale_sum_ref[...]
    high = value.astype(jnp.bfloat16).astype(jnp.float32)
    lane = lax.broadcasted_iota(jnp.int32, (value.shape[0], LANES), 1)
    first = lane_ref[0]
    lanes = jnp.where(lane == first, high, jnp.where(lane == first + 1, value - high, 0.0))
    write(slice(width, width + LANES), lanes)
    for i in (count - 2, count - 1):
        for k in range(3):
            act_copy(i, k).wait()
    scaled_copy.wait()


class Unit:
    def __init__(self, order, lane, pieces, parts, weights):
        size = pieces[0].shape[0]
        rows = size * len(pieces)
        units, width = weights[0].shape
        count = units // F_BLOCK
        anywhere = pl.BlockSpec(memory_space=pl.ANY)
        inside = pl.BlockSpec(memory_space=pltpu.VMEM)
        scalar = pl.BlockSpec(memory_space=pltpu.SMEM)
        bf16 = jnp.bfloat16
        out = order.call(
            functools.partial(unit_kernel, len(pieces), parts, count),
            [lane, *pieces, *weights],
            [scalar] + [anywhere] * (len(pieces) + 3),
            [jax.ShapeDtypeStruct((rows, units), bf16)] * 3
            + [jax.ShapeDtypeStruct((rows, width), bf16)]
            + [jax.ShapeDtypeStruct((part, width + LANES), bf16) for part in parts],
            [anywhere] * 4 + [inside] * len(parts),
            scratch_shapes=[
                pltpu.VMEM((rows, width), bf16),
                pltpu.VMEM((rows, width), bf16),
                pltpu.VMEM((rows, LANES), bf16),
                pltpu.VMEM((rows, width), bf16),
                pltpu.VMEM((rows, width), jnp.float32),
                pltpu.VMEM((rows, 1), jnp.float32),
                pltpu.VMEM((4, 3, F_BLOCK, width), bf16),
                pltpu.VMEM((2, 3, rows, F_BLOCK), bf16),
                pltpu.SemaphoreType.DMA((len(pieces), 3)),
                pltpu.SemaphoreType.DMA((4, 3)),
                pltpu.SemaphoreType.DMA((2, 3)),
                pltpu.SemaphoreType.DMA(()),
            ],
        )
        self.hidden, self.gate_grad, self.up_grad, self.scaled = out[:4]
        self.partials = out[4:]
        self.pieces = pieces


def weight_kernel(n_right, n_left, n_out, *refs):
    right, refs = refs[:n_right], refs[n_right:]
    left, refs = refs[: n_left * n_out], refs[n_left * n_out :]
    out_refs, (rows_ref, sems) = refs[:n_out], refs[n_out:]
    width = rows_ref.shape[1]

    @pl.when(pl.program_id(0) == 0)
    def _():
        copies, start = [], 0
        for i, ref in enumerate(right):
            size = ref.shape[0]
            copies.append(
                pltpu.make_async_copy(
                    ref.at[:, pl.ds(0, width)], rows_ref.at[pl.ds(start, size), :], sems.at[i]
                )
            )
            start += size
        for copy in copies:
            copy.start()
        for copy in copies:
            copy.wait()

    tile = 1024
    for k, out_ref in enumerate(out_refs):
        both = jnp.concatenate([ref[...] for ref in left[k * n_left : (k + 1) * n_left]], axis=0)
        for start in range(0, width, tile):
            at = slice(start, start + tile)
            out_ref[:, at] = tn_dot(both, rows_ref[:, at]).astype(jnp.bfloat16)


def weight_grads(order, right, lefts, width):
    left = [a for one in lefts for a in one]
    rows = sum(a.shape[0] for a in lefts[0])
    units = left[0].shape[1]
    anywhere = pl.BlockSpec(memory_space=pl.ANY)
    return order.call(
        functools.partial(weight_kernel, len(right), len(lefts[0]), len(lefts)),
        [*right, *left],
        [anywhere] * len(right)
        + [pl.BlockSpec((a.shape[0], F_BLOCK), lambda i: (0, i)) for a in left],
        [jax.ShapeDtypeStruct((units, width), jnp.bfloat16)] * len(lefts),
        [pl.BlockSpec((F_BLOCK, width), lambda i: (i, 0))] * len(lefts),
        grid=(units // F_BLOCK,),
        scratch_shapes=[
            pltpu.VMEM((rows, width), jnp.bfloat16),
            pltpu.SemaphoreType.DMA((len(right),)),
        ],
    )


def unpack_kernel(slot_ref, *refs):
    grads_ref, scale_ref = refs[-2:]
    width = grads_ref.shape[1]
    slot = as_column(slot_ref[...])
    total = jnp.zeros((slot.shape[0], width + LANES), jnp.float32)
    for group, ref in enumerate(refs[:-2]):
        size = ref.shape[0]
        at = lax.broadcasted_iota(jnp.int32, (slot.shape[0], size), 1) + group * size
        placing = (at == slot).astype(jnp.float32).astype(jnp.bfloat16)
        total += jnp.dot(placing, ref[...], preferred_element_type=jnp.float32)
    grads_ref[...] = total[:, :width].astype(jnp.bfloat16)
    ones = jnp.ones((8, LANES), jnp.bfloat16)
    scale_ref[...] = nt_dot(ones, total[:, width:].astype(jnp.bfloat16))[0:1, :]


def unpack(order, slot, groups, width):
    rows = slot.shape[1]
    inside = pl.BlockSpec(memory_space=pltpu.VMEM)
    return order.call(
        unpack_kernel,
        [slot, *groups],
        [inside] * (1 + len(groups)),
        [
            jax.ShapeDtypeStruct((rows, width), jnp.bfloat16),
            jax.ShapeDtypeStruct((1, rows), jnp.float32),
        ],
        [inside] * 2,
    )


def line_device(token_rows, row_grads, gate_scale, routing, gate_weight, up_weight, down_weight):
    width = token_rows.shape[1]
    local_rows = token_rows.shape[0]
    size = 3 * local_rows // 8
    z, e, x = (lax.axis_index(name) for name in ("dp", "expert", "etensor"))
    middle = (z == 1) | (z == 2)
    w_gate, w_up, w_down = gate_weight[0], up_weight[0], down_weight[0]
    lane = ((z * 2 + x) * 2).astype(jnp.int32).reshape(1)

    slot, *groups = pack(
        e.astype(jnp.int32).reshape(1),
        x.astype(jnp.int32).reshape(1),
        routing.reshape(1, local_rows),
        gate_scale.reshape(1, local_rows),
        token_rows,
        row_grads,
        size,
    )

    def over_expert(a, g, cross=0):
        pairs = []
        for i in range(4):
            for j in range(2):
                d = (j ^ (g >> 1)) + 2 * (g & 1)
                pairs.append((i * 2 + j, (i ^ d) * 2 + (j ^ cross)))
        return lax.ppermute(a, ("expert", "etensor"), pairs)

    def along(a, pairs):
        return lax.ppermute(a, "dp", pairs)

    def across(a):
        return lax.ppermute(a, "etensor", ((0, 1), (1, 0)))

    near, far, near_other, far_other = (over_expert(a, g) for g, a in enumerate(groups))

    order = Order()
    flag = middle.astype(jnp.int32).reshape(1)
    weights = (w_gate, w_up, w_down)
    pair = 2 * size
    near_1 = along(near, PAIRS[1])
    middle_near = along(near, MIDDLE)
    order.wait(near_1, middle_near, near_other, far)
    second_near = along(near_1, MIDDLE)
    out_near = along(middle_near, OUT)
    swap_1 = across(near_1)
    (near_2,) = choose(order, flag, [(second_near, out_near)])
    out_second = along(second_near, OUT)
    swap_2 = across(near_2)
    near_3, far_copy = choose(order, flag, [(middle_near, out_second)], [far], [swap_1, far_other])
    swap_3 = across(near_3)
    far_3 = along(far_copy, PAIRS[3])
    far_1 = along(far_copy, PAIRS[1])
    u0 = Unit(order, lane, [near, near_other, far, far_other], [pair, size, size], weights)
    far_3, far_1, far_copy = choose(order, flag, [], [far_3, far_1, far], [swap_2])
    far_swap_3 = across(far_3)
    far_swap_1 = across(far_1)
    far_2 = along(far_copy, PAIRS[2])
    u1 = Unit(
        order, lane, [near_1, swap_1, near_2, swap_2, near_3, swap_3], [pair, pair, pair], weights
    )
    (far_2,) = choose(order, flag, [], [far_2], [far_swap_3])
    far_swap_2 = across(far_2)
    near_terms = [along(a, PAIRS[k + 1]) for k, a in enumerate(u1.partials)]
    u2 = Unit(order, lane, [far_3, far_1, far_swap_3, far_swap_1], [pair, pair], weights)
    others = across(u2.partials[1])
    order.wait(near_terms[0], near_terms[2])
    u3 = Unit(order, lane, [far_2, far_swap_2], [size, size], weights)
    other_2 = across(u3.partials[1])
    part_3, part_1 = sums(
        order, [u2.partials[0], others], size, [[(0, 0), (1, 0)]], [[(0, size), (1, size)]]
    )
    far_terms = [along(part_3, PAIRS[3]), along(part_1, PAIRS[1])]
    (part_2,) = sums(order, [u3.partials[0], other_2], size, [[(0, 0), (1, 0)]])
    far_terms.append(along(part_2, PAIRS[2]))
    terms = range(4)
    near_own, rest = sums(
        order,
        [u0.partials[0], *near_terms, u0.partials[2]],
        size,
        [[(k, 0) for k in terms]],
        [[(k, size) for k in terms], [(4, 0)]],
    )
    rest = across(rest)

    units_of = (u0, u1, u2, u3)
    rows = [piece for u in units_of for piece in u.pieces]
    scaled = [u.scaled for u in units_of]
    width = token_rows.shape[1]

    def grads_of(right, *names):
        lefts = [[getattr(u, name) for u in units_of] for name in names]
        return weight_grads(order, right, lefts, width)

    grad_gate, grad_up = grads_of(rows, "gate_grad", "up_grad")
    near_own, far_own = sums(
        order,
        [near_own, rest, u0.partials[1], *far_terms],
        size,
        [[(0, 0), (1, 0)]],
        [[(1, size), *[(k, 0) for k in range(2, 6)]]],
    )
    far_back = [over_expert(far_own, 1), over_expert(far_own, 1, 1)]
    near_back = [over_expert(near_own, 0), over_expert(near_own, 0, 1)]
    (grad_down,) = grads_of(scaled, "hidden")
    input_grads, scale_grads = unpack(
        order, slot, [near_back[0], far_back[0], near_back[1], far_back[1]], width
    )
    return (input_grads, scale_grads[0], grad_gate[None], grad_up[None], grad_down[None])


def plain_device(token_rows, row_grads, gate_scale, routing, gate_weight, up_weight, down_weight):
    experts = lax.axis_size("expert")
    width = token_rows.shape[1]
    local_rows = token_rows.shape[0]
    capacity = 3 * local_rows // 8
    route = routing[:, 0]
    hits = (route[:, None] == jnp.arange(experts, dtype=jnp.int32)[None, :]).astype(jnp.int32)
    before = jnp.cumsum(hits, axis=0) - hits
    slot_pos = route * capacity + jnp.sum(before * hits, axis=1)
    placing = (
        jnp.arange(experts * capacity, dtype=jnp.int32)[:, None] == slot_pos[None, :]
    ).astype(jnp.bfloat16)
    send_rows = (
        jnp.dot(placing, token_rows, preferred_element_type=jnp.float32)
        .astype(jnp.bfloat16)
        .reshape(experts, capacity, width)
    )
    send_grads = (
        jnp.dot(placing, row_grads, preferred_element_type=jnp.float32)
        .astype(jnp.bfloat16)
        .reshape(experts, capacity, width)
    )
    send_scale = (
        jnp.dot(placing, gate_scale, preferred_element_type=jnp.float32)
        .astype(jnp.bfloat16)
        .reshape(experts, capacity)
    )
    recv_rows, recv_grads, recv_scale = (
        lax.all_to_all(send_rows, "expert", split_axis=0, concat_axis=0, tiled=True),
        lax.all_to_all(send_grads, "expert", split_axis=0, concat_axis=0, tiled=True),
        lax.all_to_all(send_scale, "expert", split_axis=0, concat_axis=0, tiled=True),
    )
    group_rows, group_grads, group_scale = (
        lax.all_gather(recv_rows.reshape(-1, width), "dp", axis=0, tiled=True),
        lax.all_gather(recv_grads.reshape(-1, width), "dp", axis=0, tiled=True),
        lax.all_gather(recv_scale.reshape(-1), "dp", axis=0, tiled=True),
    )
    w_gate = gate_weight[0]
    w_up = up_weight[0]
    w_down = down_weight[0]
    scale_column = group_scale.astype(jnp.float32)[:, None]
    gate_pre = jnp.einsum("rd,fd->rf", group_rows, w_gate, preferred_element_type=jnp.float32)
    up_pre = jnp.einsum("rd,fd->rf", group_rows, w_up, preferred_element_type=jnp.float32)
    sigmoid_gate = jax.nn.sigmoid(gate_pre)
    activated = gate_pre * sigmoid_gate
    hidden = (activated * up_pre).astype(jnp.bfloat16)
    hidden_raw = jnp.einsum("rd,fd->rf", group_grads, w_down, preferred_element_type=jnp.float32)
    scale_term = jnp.sum(hidden.astype(jnp.float32) * hidden_raw, axis=1)
    hidden_grad = scale_column * hidden_raw
    gate_pre_grad = (
        hidden_grad * up_pre * sigmoid_gate * (1.0 + gate_pre * (1.0 - sigmoid_gate))
    ).astype(jnp.bfloat16)
    up_pre_grad = (hidden_grad * activated).astype(jnp.bfloat16)
    scaled_grads = (scale_column * group_grads.astype(jnp.float32)).astype(jnp.bfloat16)
    grad_gate = jnp.einsum(
        "rf,rd->fd", gate_pre_grad, group_rows, preferred_element_type=jnp.float32
    ).astype(jnp.bfloat16)
    grad_up = jnp.einsum(
        "rf,rd->fd", up_pre_grad, group_rows, preferred_element_type=jnp.float32
    ).astype(jnp.bfloat16)
    grad_down = jnp.einsum(
        "rf,rd->fd", hidden, scaled_grads, preferred_element_type=jnp.float32
    ).astype(jnp.bfloat16)
    row_term = jnp.dot(gate_pre_grad, w_gate, preferred_element_type=jnp.float32) + jnp.dot(
        up_pre_grad, w_up, preferred_element_type=jnp.float32
    )
    share_total, share_scale = (
        lax.psum_scatter(row_term, ("dp", "etensor"), scatter_dimension=0, tiled=True),
        lax.psum_scatter(scale_term, ("dp", "etensor"), scatter_dimension=0, tiled=True),
    )
    row_total, scale_total = (
        lax.all_gather(share_total, "etensor", axis=0, tiled=True),
        lax.all_gather(share_scale, "etensor", axis=0, tiled=True),
    )
    back_rows, back_scale = (
        lax.all_to_all(
            row_total.reshape(experts, capacity, width),
            "expert",
            split_axis=0,
            concat_axis=0,
            tiled=True,
        ),
        lax.all_to_all(
            scale_total.reshape(experts, capacity),
            "expert",
            split_axis=0,
            concat_axis=0,
            tiled=True,
        ),
    )
    input_grads = jnp.take(back_rows.reshape(-1, width), slot_pos, axis=0).astype(jnp.bfloat16)
    scale_grads = jnp.take(back_scale.reshape(-1), slot_pos, axis=0)
    return (input_grads, scale_grads, grad_gate[None], grad_up[None], grad_down[None])


def solution(mesh):
    in_specs = (
        P(("dp", "expert"), None),
        P(("dp", "expert"), None),
        P(("dp", "expert")),
        P(("dp", "expert"), None),
        P("expert", ("dp", "etensor"), None),
        P("expert", ("dp", "etensor"), None),
        P("expert", ("dp", "etensor"), None),
    )
    out_specs = (
        P(("dp", "expert"), None),
        P(("dp", "expert")),
        P("expert", ("dp", "etensor"), None),
        P("expert", ("dp", "etensor"), None),
        P("expert", ("dp", "etensor"), None),
    )
    sizes = (mesh.shape["dp"], mesh.shape["expert"], mesh.shape["etensor"])
    per_device = line_device if sizes == (4, 4, 2) else plain_device
    return jax.shard_map(
        per_device, mesh=mesh, in_specs=in_specs, out_specs=out_specs, check_vma=False
    )
```
